32 devices in a mesh: dp: 4 (over x, core), tensor: 8 (over z, y).
Axes of the slice: x: 2, y: 2, z: 4, core: 2. Of those that a mesh axis runs over, the one named last changes fastest.
Arguments:
- tokens: bfloat16 [4096, 3072], P(('dp', 'tensor')), may hold values from -6 to 6
- routes: int32 [4096, 2], P(('dp', 'tensor')), may hold values from 0 to 7, as said below
- router: bfloat16 [3072, 8], replicated, may hold values from -0.109375 to 0.109375
- w_up: bfloat16 [3072, 16384], P('dp', 'tensor'), may hold values from -0.109375 to 0.109375
- w_down: bfloat16 [16384, 3072], P(('tensor', 'dp')), may hold values from -0.046875 to 0.046875
- grad_parts: bfloat16 [4, 16384, 3072], P('dp', 'tensor'), may hold values from -6 to 6
- master: float32 [16384, 3072], P(('tensor', 'dp')), may hold values from -4 to 4
- moment_one: bfloat16 [16384, 3072], P(('tensor', 'dp')), may hold values from -3 to 3
- moment_two: float32 [16384, 3072], P(('tensor', 'dp')), may hold values from 0.01 to 1
Outputs:
- mixed: bfloat16 [4096, 3072], P(('dp', 'tensor'))
- new_master: float32 [16384, 3072], P(('tensor', 'dp'))
- new_moment_one: bfloat16 [16384, 3072], P(('tensor', 'dp'))
- new_moment_two: float32 [16384, 3072], P(('tensor', 'dp'))
The draws below stay inside these ranges and needn't reach their ends.
Inputs may be any that keep to these rules, and one draw needn't show every extreme that they name: `routes`: each row names two different experts. Among the 128 rows of one device at most 48 name expert 0, and on some device exactly 48.
All inputs are finite; a program needn't handle non-finite values.
Results may differ from the reference program's by a relative error of at most 0.02.
Values may be sent and summed in bfloat16 or wider, within the bound.
A program may use at most 128 MiB of HBM per device.

```python
import math
import jax
import jax.numpy as jnp
from jax import lax

D = 3072
FF = 16384
EXPERTS = 8
TOK_DEV = 128
CAP = 48
TOKENS = 4096
N_DP = 4
N_TENSOR = 8


def draw_routes(key, part):
    key = jax.random.fold_in(key, 7)
    key_count, key_order, key_partner, key_other, key_swap = jax.random.split(key, 5)
    blocks = TOKENS // TOK_DEV
    counts = jax.random.randint(key_count, (blocks,), CAP // 2, CAP + 1)
    counts = counts.at[0].set(CAP)

    def shuffled(one_key):
        return jax.random.permutation(one_key, TOK_DEV)
    rank_table = jax.vmap(shuffled)(jax.random.split(key_order, blocks))
    routed = (rank_table < counts[:, None]).reshape(TOKENS)
    partner = jax.random.randint(key_partner, (TOKENS,), 1, EXPERTS)
    offset_draw = jax.random.randint(key_other, (TOKENS,), 1, EXPERTS - 1)
    second = 1 + (partner - 1 + offset_draw) % (EXPERTS - 1)
    leading = jnp.where(routed, 0, partner)
    trailing = jnp.where(routed, partner, second)
    swapped = jax.random.randint(key_swap, (TOKENS,), 0, 2) == 1
    first_col = jnp.where(swapped, trailing, leading)
    second_col = jnp.where(swapped, leading, trailing)
    return jnp.stack([first_col, second_col], axis=1).astype(jnp.int32)


def strengthened(result, own_key, source, target, parts, factor):
    def block_of(axis_at):
        return (jnp.arange(result.shape[axis_at]) // (result.shape[axis_at] // parts)).reshape((-1,) + (1,) * (result.ndim - 1 - axis_at))

    one_side = jax.random.permutation(own_key, parts)[block_of(target)]
    second = (block_of(target) + parts // 2) % parts
    return jnp.where((block_of(source) == one_side) | (block_of(source) == second), factor * result, result)


def level_of(own_key, shape, cuts, smallest, top_value):
    loudness = 1.0
    for position, blocks in cuts:
        heights = jax.random.uniform(jax.random.fold_in(jax.random.fold_in(own_key, 6), position), (blocks,), jnp.float32, smallest / len(cuts), top_value / len(cuts))
        loudness = loudness * jnp.repeat(jnp.exp(heights), shape[position] // blocks).reshape((-1,) + (1,) * (len(shape) - 1 - position))
    return loudness


def gaussian(own_key, shape, scale, most, shards=(), held_as=jnp.bfloat16):
    factor_of = level_of(own_key, shape, shards, -0.22, 0.18) if shards else 1.0
    values = jax.random.normal(own_key, shape, jnp.float32) * scale * factor_of
    return jnp.minimum(jnp.maximum(values, -most), most).astype(held_as)


def noise_with(own_key, shape, deviation, most, cuts, heavy, held_as=jnp.bfloat16):
    values = deviation * jax.random.normal(own_key, shape, jnp.float32)
    if cuts:
        values = values * level_of(own_key, shape, cuts, -0.22, 0.18)
    return jnp.clip(strengthened(values, jax.random.fold_in(own_key, 3), *heavy), -most, most).astype(held_as)


def setup_inputs(seed: int = 0) -> dict:
    seeds = jax.random.split(jax.random.key(seed), 10)
    return {
        "tokens": gaussian(seeds[0], (TOKENS, D), 1.0, 6.0, ((0, 32),)),
        "routes": draw_routes(jax.random.fold_in(seeds[9], 71), 0),
        "router": gaussian(seeds[2], (D, EXPERTS), D ** -0.5, 0.109375),
        "w_up": gaussian(seeds[3], (D, FF), D ** -0.5, 0.109375, ((0, 4), (1, 8))),
        "w_down": gaussian(seeds[4], (FF, D), FF ** -0.5, 0.046875, ((0, 32),)),
        "grad_parts": noise_with(seeds[5], (N_DP, FF, D), 1.0, 6.0, ((0, 4), (1, 8)), (0, 1, 4, 2.0)),
        "master": gaussian(seeds[6], (FF, D), 0.5, 4.0, ((0, 32),), jnp.float32),
        "moment_one": gaussian(seeds[7], (FF, D), 0.3, 3.0, ((0, 32),)),
        "moment_two": jnp.clip(jnp.exp(math.log(1.0) - 4.6051702 * jax.random.uniform(seeds[8], (FF, D), jnp.float32) ** level_of(seeds[8], (FF, D), ((0, 32),), -0.2, 0.2)), 0.01, 1.0),
    }


beta_first = 0.9
beta_second = 0.999
learn_rate = 0.01
decay_rate = 0.1
adam_eps = 1e-08
bias_first = 1.0 - (0.9 ** 10) ** 10
bias_second = 1.0 - (0.999 ** 10) ** 10

def gating_of(tokens, routes, router):
    logits = jnp.dot(tokens, router, preferred_element_type=jnp.float32)
    expert_iota = jnp.arange(logits.shape[1], dtype=jnp.int32)
    chosen = lax.optimization_barrier(jnp.sum(jnp.where(routes[:, :, None] == expert_iota, logits[:, None, :], 0.0), axis=2))
    is_first = routes[:, 0] == 0
    routed = is_first | (routes[:, 1] == 0)
    own_logit = jnp.where(is_first, chosen[:, 0], chosen[:, 1])
    partner = jnp.where(is_first, chosen[:, 1], chosen[:, 0])
    gating = jnp.where(routed, jax.nn.sigmoid(own_logit - partner), 0.0)
    return (routed, gating)

def adam_step(grad_total, master, moment_one, moment_two):
    new_one = (beta_first * moment_one.astype(jnp.float32) + (1.0 - beta_first) * grad_total).astype(jnp.bfloat16)
    new_two = beta_second * moment_two + (1.0 - beta_second) * grad_total * grad_total
    update = new_one.astype(jnp.float32) / bias_first / (jnp.sqrt(new_two / bias_second) + adam_eps)
    new_master = master - learn_rate * (update + decay_rate * master)
    return (new_master, new_one, new_two)

def reference(tokens, routes, router, w_up, w_down, grad_parts, master, moment_one, moment_two):
    routed, gating = gating_of(tokens, routes, router)
    blocks = N_DP * N_TENSOR
    routed_blocks = routed.reshape(blocks, TOK_DEV)
    slot_index = (jnp.cumsum(routed_blocks.astype(jnp.int32), axis=1) - 1).astype(jnp.int32)
    width = FF // N_TENSOR

    def place(block_tokens, block_target):
        return jnp.zeros((CAP, D), block_tokens.dtype).at[block_target].set(block_tokens, mode='drop')

    def fetch(out_rows, slots):
        return jnp.take(out_rows, jnp.clip(slots, 0, CAP - 1), axis=0)

    def group_forward(inputs):
        group_tokens, group_slots, group_routed, group_gating = inputs
        target = jnp.where(group_routed, group_slots, CAP).astype(jnp.int32)
        dispatched = jax.vmap(place)(group_tokens, target).reshape(N_TENSOR * CAP, D)
        up_out = jnp.dot(dispatched, w_up, preferred_element_type=jnp.float32)
        hidden = jax.nn.gelu(up_out, approximate=False).astype(jnp.bfloat16)

        def add_group(running, group_number):
            offset = (group_number * width).astype(jnp.int32)
            hid_cols = lax.dynamic_slice_in_dim(hidden, offset, width, 1)
            rows_part = lax.dynamic_slice_in_dim(w_down, offset, width, 0)
            term = jnp.dot(hid_cols, rows_part, preferred_element_type=jnp.float32).astype(jnp.bfloat16)
            term = lax.optimization_barrier(term)
            return (running + term.astype(jnp.float32), None)
        summed, _ = lax.scan(add_group, jnp.zeros((N_TENSOR * CAP, D), jnp.float32), jnp.arange(N_TENSOR, dtype=jnp.int32))
        summed = summed.reshape(N_TENSOR, CAP, D)
        picked = jax.vmap(fetch)(summed, group_slots)
        return (picked * group_gating[:, :, None]).astype(jnp.bfloat16)
    mixed = lax.map(group_forward, (tokens.reshape(N_DP, N_TENSOR, TOK_DEV, D), slot_index.reshape(N_DP, N_TENSOR, TOK_DEV), routed_blocks.reshape(N_DP, N_TENSOR, TOK_DEV), gating.reshape(N_DP, N_TENSOR, TOK_DEV)))
    mixed = mixed.reshape(TOKENS, D)
    grad_total = lax.optimization_barrier(jnp.sum(grad_parts.astype(jnp.float32), axis=0))
    new_master, new_one, new_two = adam_step(grad_total, master, moment_one, moment_two)
    return (mixed, new_master, new_one, new_two)
```

```python
import functools

import jax
import jax.numpy as jnp
from jax import lax
from jax.experimental import pallas as pl
from jax.experimental.pallas import tpu as pltpu
from jax.sharding import PartitionSpec as P

CAP = 48


beta_first = 0.9
beta_second = 0.999
learn_rate = 0.01
decay_rate = 0.1
adam_eps = 1e-08
bias_first = 1.0 - (0.9**10) ** 10
bias_second = 1.0 - (0.999**10) ** 10


def gating_of(tokens, routes, router):
    logits = jnp.dot(tokens, router, preferred_element_type=jnp.float32)
    expert_iota = jnp.arange(logits.shape[1], dtype=jnp.int32)
    chosen = jnp.sum(jnp.where(routes[:, :, None] == expert_iota, logits[:, None, :], 0.0), axis=2)
    is_first = routes[:, 0] == 0
    routed = is_first | (routes[:, 1] == 0)
    own_logit = jnp.where(is_first, chosen[:, 0], chosen[:, 1])
    partner = jnp.where(is_first, chosen[:, 1], chosen[:, 0])
    gating = jnp.where(routed, jax.nn.sigmoid(own_logit - partner), 0.0)
    return (routed, gating)


def adam_step(grad_total, master, moment_one, moment_two):
    new_one = (
        beta_first * moment_one.astype(jnp.float32) + (1.0 - beta_first) * grad_total
    ).astype(jnp.bfloat16)
    new_two = beta_second * moment_two + (1.0 - beta_second) * grad_total * grad_total
    update = new_one.astype(jnp.float32) / bias_first / (jnp.sqrt(new_two / bias_second) + adam_eps)
    new_master = master - learn_rate * (update + decay_rate * master)
    return (new_master, new_one, new_two)


def local(tokens, routes, router, w_up, w_down, grad_parts, master, moment_one, moment_two):
    routed, gating = gating_of(tokens, routes, router)
    slot_index = jnp.cumsum(routed.astype(jnp.int32)) - 1
    slot_iota = jnp.arange(CAP, dtype=jnp.int32)
    picks = ((slot_index[None, :] == slot_iota[:, None]) & routed[None, :]).astype(jnp.bfloat16)
    picked_rows = jnp.dot(picks, tokens, preferred_element_type=jnp.float32).astype(jnp.bfloat16)
    gathered = lax.all_gather(picked_rows, "tensor", axis=0, tiled=True)
    up_out = jnp.dot(
        gathered, lax.all_gather(w_up, "dp", axis=0, tiled=True), preferred_element_type=jnp.float32
    )
    hidden = jax.nn.gelu(up_out, approximate=False).astype(jnp.bfloat16)
    partials = jnp.dot(
        hidden, lax.all_gather(w_down, "dp", axis=0, tiled=True), preferred_element_type=jnp.float32
    )
    owned = lax.psum_scatter(
        partials.astype(jnp.bfloat16), "tensor", scatter_dimension=0, tiled=True
    ).astype(jnp.float32)
    combined = jnp.take(owned, jnp.clip(slot_index, 0, CAP - 1), axis=0)
    mixed = (combined * gating[:, None]).astype(jnp.bfloat16)
    local_grad = grad_parts[0]
    grad_total = lax.psum_scatter(local_grad, "dp", scatter_dimension=0, tiled=True).astype(
        jnp.float32
    )
    new_master, new_one, new_two = adam_step(grad_total, master, moment_one, moment_two)
    return (mixed, new_master, new_one, new_two)


CHUNKS = 8
VMEM_BYTES = 60 * 1024 * 1024


def flip(index, bit):
    return index + bit - 2 * bit * lax.rem(lax.div(index, bit), 2)


def layer_kernel(
    n_dp, n_tensor, pk, wup_hbm, wdown_hbm, grad_hbm,
    owned, gsum,
    x, wup, up, up_near, up_cross, hid, wd, out, from_y, from_z, from_far, fin_out, fin_in,
    g_own, g_near, g_cross, send_sem, recv_sem, local_sem,
):
    p = lax.axis_index("dp")
    t = lax.axis_index("tensor")
    c, h = lax.rem(p, 2), lax.div(p, 2)
    z, y = lax.div(t, 2), lax.rem(t, 2)
    p1, p2 = flip(p, 1), flip(p, 2)
    p3 = flip(p1, 2)
    t1, t2, t4 = flip(t, 1), flip(t, 2), flip(t, 4)
    z1, z2 = flip(z, 1), flip(z, 2)
    z3 = flip(z1, 2)
    core, cross, diag = (p1, t), (p2, t), (p3, t)
    side, near, far = (p, t1), (p, t2), (p, t4)
    cap = pk.shape[1]
    share = wdown_hbm.shape[0]
    piece = share // CHUNKS
    n_z = n_tensor // 2
    used = [0]
    sent = []

    def send(src, dst, device):
        k = used[0]
        used[0] += 1
        copy = pltpu.make_async_remote_copy(
            src_ref=src, dst_ref=dst, send_sem=send_sem.at[k], recv_sem=recv_sem.at[k],
            device_id=device, device_id_type=pl.DeviceIdType.MESH,
        )
        copy.start()
        sent.append(copy)
        return copy

    barrier = pltpu.get_barrier_semaphore()
    for device in (core, cross, diag, side, near, far):
        pl.semaphore_signal(barrier, inc=1, device_id=device, device_id_type=pl.DeviceIdType.MESH)
    pl.semaphore_wait(barrier, 6)

    def rows_of(q):
        return pl.ds(pl.multiple_of(q * cap, 16), cap)

    def share_of(q):
        return pl.ds(pl.multiple_of(q * share, 16), share)

    tok = [
        send(pk.at[p2], x.at[t, rows_of(p)], cross),
        send(pk.at[p3], x.at[t, rows_of(p)], diag),
        send(pk.at[p1], x.at[t, rows_of(p)], core),
    ]
    loads = [
        pltpu.make_async_copy(pk.at[p], x.at[t, rows_of(p)], local_sem.at[0]),
        pltpu.make_async_copy(wup_hbm, wup, local_sem.at[1]),
        pltpu.make_async_copy(grad_hbm.at[0, share_of(p2)], g_own.at[0], local_sem.at[2]),
        pltpu.make_async_copy(wdown_hbm, wd.at[c], local_sem.at[3]),
        pltpu.make_async_copy(grad_hbm.at[0, share_of(p)], g_own.at[1], local_sem.at[4]),
    ]
    for load in loads:
        load.start()
    grad_core = [send(grad_hbm.at[0, share_of(p3)], g_near.at[0], core)]

    for copy in tok:
        copy.wait_recv()
    loads[0].wait()

    def pass_on(block, devices):
        return [send(x.at[block], x.at[block], device) for device in devices]

    tile = 512

    def project(from_z_at, s):
        block = 2 * from_z_at + (y if s == 1 else 1 - y)

        @pl.loop(0, 2)
        def _(part):
            for j in range(up.shape[5] // tile):
                start = pl.multiple_of(part * up.shape[5] + j * tile, tile)
                res = jnp.dot(x[block], wup[:, pl.ds(start, tile)], preferred_element_type=jnp.float32)
                res = res.astype(jnp.bfloat16)
                for q in range(n_dp):
                    up[part, q, s, from_z_at, :, j * tile : (j + 1) * tile] = res[
                        q * cap : (q + 1) * cap
                    ]

    def up_to_core(s):
        return [send(up.at[:, 1 - c + 2 * a, s], up_near.at[a, s], core) for a in range(2)]

    def up_to_cross(s):
        @pl.loop(0, n_z)
        def _(m):
            for a in range(2):
                total = up[1 - h, c + 2 * a, s, m].astype(jnp.float32) + up_near[
                    a, s, 1 - h, m
                ].astype(jnp.float32)
                up[1 - h, c + 2 * a, s, m] = total.astype(jnp.bfloat16)

        return [send(up.at[1 - h, c + 2 * a, s], up_cross.at[a, s], cross) for a in range(2)]

    step = 32

    def pair_sum(first, end):
        @pl.loop(first * (piece // step), end * (piece // step))
        def _(i):
            rows = pl.ds(pl.multiple_of(i * step, step), step)
            total = g_own[0, rows].astype(jnp.float32) + g_near[0, rows].astype(jnp.float32)
            g_own[0, rows] = total.astype(jnp.bfloat16)

    def send_grad(k):
        rows = pl.ds(k * piece, piece)
        return send(g_own.at[0, rows], g_cross.at[rows], cross)

    own_far, own_near, own_side = pass_on(t, (far, near, side))
    loads[1].wait()
    project(z, 1)
    own_far.wait_recv()
    far_near, far_side = pass_on(t4, (near, side))
    project(z2, 1)
    own_near.wait_recv()
    (near_side,) = pass_on(t2, (side,))
    project(z1, 1)
    far_near.wait_recv()
    (both_side,) = pass_on(flip(t2, 4), (side,))
    project(z3, 1)

    core_own = up_to_core(1)
    loads[2].wait()
    grad_core[0].wait_recv()
    pair_sum(0, 1)
    grad_cross = [send_grad(0)]
    own_side.wait_recv()
    project(z, 0)
    for copy in core_own:
        copy.wait_recv()
    cross_own = up_to_cross(1)
    for copy, at in ((far_side, z2), (near_side, z1), (both_side, z3)):
        copy.wait_recv()
        project(at, 0)
    core_other = up_to_core(0)
    wd_core = send(wdown_hbm, wd.at[c], core)
    grad_core.append(send(grad_hbm.at[0, share_of(p1)], g_near.at[1], core))
    for copy in core_other:
        copy.wait_recv()
    cross_other = up_to_cross(0)

    pair_sum(1, CHUNKS)

    loads[3].wait()
    wd_core.wait_recv()
    width = 256

    def expert(s):
        @pl.loop(0, n_z)
        def _(m):
            for a in range(2):
                pre = (
                    up[h, c + 2 * a, s, m].astype(jnp.float32)
                    + up_near[a, s, h, m].astype(jnp.float32)
                    + up_cross[a, s, m].astype(jnp.float32)
                )
                act = 0.5 * pre * (1.0 + lax.erf(pre * 0.7071067811865476))
                hid[rows_of(2 * m + a), :] = act.astype(jnp.bfloat16)

        @pl.loop(0, out.shape[4] // width)
        def _(j):
            cols = pl.ds(pl.multiple_of(j * width, width), width)
            weight = wd[:, :, cols].reshape(2 * share, width)
            res = jnp.dot(hid[...], weight, preferred_element_type=jnp.float32)
            out[s, :, :, :, cols] = res.reshape(n_z, 2, cap, width).astype(jnp.bfloat16)

    for copy in cross_own:
        copy.wait_recv()
    expert(1)
    for copy in cross_other:
        copy.wait_recv()
    for k in range(1, CHUNKS):
        grad_cross.append(send_grad(k))
    expert(0)

    y_copies = [
        send(out.at[0, at], from_y.at[slot], side) for slot, at in enumerate((z3, z2, z1, z))
    ]
    loads[4].wait()
    grad_core[1].wait_recv()

    def finish_grad(k):
        grad_cross[k].wait_recv()

        @pl.loop(0, piece // step)
        def _(i):
            rows = pl.ds(pl.multiple_of(k * piece + i * step, step), step)
            total = (
                g_own[1, rows].astype(jnp.float32)
                + g_near[1, rows].astype(jnp.float32)
                + g_cross[rows].astype(jnp.float32)
            )
            gsum[rows, :] = total.astype(jnp.bfloat16)

    def total_of(at, a, *others):
        total = out[1, at, a].astype(jnp.float32)
        for other in others:
            total += other[a].astype(jnp.float32)
        return total

    def merge(at, *others):
        for a in range(2):
            out[1, at, a] = total_of(at, a, *others).astype(jnp.bfloat16)

    y_copies[0].wait_recv()
    merge(z3, from_y.at[0])
    z_first = send(out.at[1, z3], from_z.at[0], near)
    y_copies[1].wait_recv()
    z_first.wait_recv()
    merge(z2, from_y.at[1], from_z.at[0])
    z_far = send(out.at[1, z2], from_far, far)
    y_copies[2].wait_recv()
    merge(z1, from_y.at[2])
    z_second = send(out.at[1, z1], from_z.at[1], near)
    for k in range(CHUNKS // 2):
        finish_grad(k)
    y_copies[3].wait_recv()
    z_second.wait_recv()
    z_far.wait_recv()
    last = (from_y.at[3], from_z.at[1], from_far)
    fin_out[...] = total_of(z, 1 - h, *last).astype(jnp.bfloat16)
    fin = send(fin_out, fin_in, cross)
    for k in range(CHUNKS // 2, CHUNKS):
        finish_grad(k)
    fin.wait_recv()
    owned[...] = total_of(z, h, *last) + fin_in[...].astype(jnp.float32)

    for copy in sent:
        copy.wait_send()
    assert used[0] == send_sem.shape[0]


def layer(n_dp, n_tensor, pk, w_up, w_down, grad_parts):
    cap, depth = pk.shape[1:]
    hidden = w_up.shape[1]
    share, model = w_down.shape
    half = jnp.bfloat16
    copies = 29 + CHUNKS
    n_z = n_tensor // 2
    scratch = [
        pltpu.VMEM((n_tensor, n_dp * cap, depth), half),
        pltpu.VMEM((depth, hidden), half),
        pltpu.VMEM((2, n_dp, 2, n_z, cap, hidden // 2), half),
        pltpu.VMEM((2, 2, 2, n_z, cap, hidden // 2), half),
        pltpu.VMEM((2, 2, n_z, cap, hidden // 2), half),
        pltpu.VMEM((2 * n_z * cap, hidden // 2), half),
        pltpu.VMEM((2, share, model), half),
        pltpu.VMEM((2, n_z, 2, cap, model), half),
        pltpu.VMEM((n_z, 2, cap, model), half),
        pltpu.VMEM((2, 2, cap, model), half),
        pltpu.VMEM((2, cap, model), half),
        pltpu.VMEM((cap, model), half),
        pltpu.VMEM((cap, model), half),
        pltpu.VMEM((2, share, model), half),
        pltpu.VMEM((2, share, model), half),
        pltpu.VMEM((share, model), half),
        pltpu.SemaphoreType.DMA((copies,)),
        pltpu.SemaphoreType.DMA((copies,)),
        pltpu.SemaphoreType.DMA((5,)),
    ]
    flops = 2 * n_tensor * n_dp * cap * depth * hidden + 2 * n_tensor * cap * hidden * model
    return pl.pallas_call(
        functools.partial(layer_kernel, n_dp, n_tensor),
        out_shape=(
            jax.ShapeDtypeStruct((cap, model), jnp.float32),
            jax.ShapeDtypeStruct((share, model), half),
        ),
        in_specs=[pl.BlockSpec(memory_space=pltpu.VMEM)] + [pl.BlockSpec(memory_space=pl.ANY)] * 3,
        out_specs=(pl.BlockSpec(memory_space=pltpu.VMEM), pl.BlockSpec(memory_space=pltpu.VMEM)),
        scratch_shapes=scratch,
        cost_estimate=pl.CostEstimate(
            flops=flops, bytes_accessed=40 * share * model, transcendentals=n_tensor * cap * hidden
        ),
        compiler_params=pltpu.CompilerParams(
            collective_id=0, has_side_effects=True, vmem_limit_bytes=VMEM_BYTES
        ),
    )(pk, w_up, w_down, grad_parts)


def local_kernel(n_dp, n_tensor, tokens, routes, router, w_up, w_down, grad_parts, master, moment_one, moment_two):
    routed, gating = gating_of(tokens, routes, router)
    slot_index = jnp.cumsum(routed.astype(jnp.int32)) - 1
    slot_iota = jnp.arange(CAP, dtype=jnp.int32)
    picks = ((slot_index[None, :] == slot_iota[:, None]) & routed[None, :]).astype(jnp.bfloat16)
    picked_rows = jnp.dot(picks, tokens, preferred_element_type=jnp.float32).astype(jnp.bfloat16)
    pk = picked_rows.reshape(CAP, n_dp, -1).transpose(1, 0, 2)
    owned, grad_total = layer(n_dp, n_tensor, pk, w_up, w_down, grad_parts)
    combined = jnp.take(owned, jnp.clip(slot_index, 0, CAP - 1), axis=0)
    mixed = (combined * gating[:, None]).astype(jnp.bfloat16)
    new_master, new_one, new_two = adam_step(
        grad_total.astype(jnp.float32), master, moment_one, moment_two
    )
    return (mixed, new_master, new_one, new_two)


def solution(mesh):
    placed = (
        P(("dp", "tensor"), None),
        P(("dp", "tensor"), None),
        P(),
        P("dp", "tensor"),
        P(("tensor", "dp"), None),
        P("dp", "tensor", None),
        P(("tensor", "dp"), None),
        P(("tensor", "dp"), None),
        P(("tensor", "dp"), None),
    )
    n_dp, n_tensor = mesh.shape["dp"], mesh.shape["tensor"]
    if (n_dp, n_tensor) == (4, 8):
        body = functools.partial(local_kernel, n_dp, n_tensor)
    else:
        body = local
    return jax.shard_map(
        body,
        mesh=mesh,
        in_specs=placed,
        out_specs=(
            P(("dp", "tensor"), None),
            P(("tensor", "dp"), None),
            P(("tensor", "dp"), None),
            P(("tensor", "dp"), None),
        ),
        check_vma=False,
    )
```

```python
import functools

import jax
import jax.numpy as jnp
from jax import lax
from jax.experimental import pallas as pl
from jax.experimental.pallas import tpu as pltpu
from jax.sharding import PartitionSpec as P

CAP = 48


beta_first = 0.9
beta_second = 0.999
learn_rate = 0.01
decay_rate = 0.1
adam_eps = 1e-08
bias_first = 1.0 - (0.9**10) ** 10
bias_second = 1.0 - (0.999**10) ** 10


def gating_of(tokens, routes, router):
    logits = jnp.dot(tokens, router, preferred_element_type=jnp.float32)
    expert_iota = jnp.arange(logits.shape[1], dtype=jnp.int32)
    chosen = jnp.sum(jnp.where(routes[:, :, None] == expert_iota, logits[:, None, :], 0.0), axis=2)
    is_first = routes[:, 0] == 0
    routed = is_first | (routes[:, 1] == 0)
    own_logit = jnp.where(is_first, chosen[:, 0], chosen[:, 1])
    partner = jnp.where(is_first, chosen[:, 1], chosen[:, 0])
    gating = jnp.where(routed, jax.nn.sigmoid(own_logit - partner), 0.0)
    return (routed, gating)


def adam_step(grad_total, master, moment_one, moment_two):
    new_one = (
        beta_first * moment_one.astype(jnp.float32) + (1.0 - beta_first) * grad_total
    ).astype(jnp.bfloat16)
    new_two = beta_second * moment_two + (1.0 - beta_second) * grad_total * grad_total
    update = new_one.astype(jnp.float32) / bias_first / (jnp.sqrt(new_two / bias_second) + adam_eps)
    new_master = master - learn_rate * (update + decay_rate * master)
    return (new_master, new_one, new_two)


def local(tokens, routes, router, w_up, w_down, grad_parts, master, moment_one, moment_two):
    routed, gating = gating_of(tokens, routes, router)
    slot_index = jnp.cumsum(routed.astype(jnp.int32)) - 1
    slot_iota = jnp.arange(CAP, dtype=jnp.int32)
    picks = ((slot_index[None, :] == slot_iota[:, None]) & routed[None, :]).astype(jnp.bfloat16)
    picked_rows = jnp.dot(picks, tokens, preferred_element_type=jnp.float32).astype(jnp.bfloat16)
    gathered = lax.all_gather(picked_rows, "tensor", axis=0, tiled=True)
    up_out = jnp.dot(
        gathered, lax.all_gather(w_up, "dp", axis=0, tiled=True), preferred_element_type=jnp.float32
    )
    hidden = jax.nn.gelu(up_out, approximate=False).astype(jnp.bfloat16)
    partials = jnp.dot(
        hidden, lax.all_gather(w_down, "dp", axis=0, tiled=True), preferred_element_type=jnp.float32
    )
    owned = lax.psum_scatter(
        partials.astype(jnp.bfloat16), "tensor", scatter_dimension=0, tiled=True
    ).astype(jnp.float32)
    combined = jnp.take(owned, jnp.clip(slot_index, 0, CAP - 1), axis=0)
    mixed = (combined * gating[:, None]).astype(jnp.bfloat16)
    local_grad = grad_parts[0]
    grad_total = lax.psum_scatter(local_grad, "dp", scatter_dimension=0, tiled=True).astype(
        jnp.float32
    )
    new_master, new_one, new_two = adam_step(grad_total, master, moment_one, moment_two)
    return (mixed, new_master, new_one, new_two)


CHUNKS = 8
VMEM_BYTES = 60 * 1024 * 1024


def flip(index, bit):
    return index + bit - 2 * bit * lax.rem(lax.div(index, bit), 2)


def layer_kernel(
    n_dp, n_tensor, pk, wup_hbm, wdown_hbm, grad_hbm,
    owned, gsum,
    x, wup, up, up_near, up_cross, hid, wd, out, from_y, from_z, from_far, fin_out, fin_in,
    g_own, g_near, g_cross, send_sem, recv_sem, local_sem,
):
    p = lax.axis_index("dp")
    t = lax.axis_index("tensor")
    c, h = lax.rem(p, 2), lax.div(p, 2)
    y, low, high = lax.rem(t, 2), lax.rem(lax.div(t, 2), 2), lax.div(t, 4)
    other = 1 - high
    p1, p2 = flip(p, 1), flip(p, 2)
    p3 = flip(p1, 2)
    t1, t2, t4 = flip(t, 1), flip(t, 2), flip(t, 4)
    core, cross, diag = (p1, t), (p2, t), (p3, t)
    side, near, far = (p, t1), (p, t2), (p, t4)
    cap = pk.shape[1]
    share = wdown_hbm.shape[0]
    piece = share // CHUNKS
    used = [0]
    sent = []

    def send(src, dst, device):
        k = used[0]
        used[0] += 1
        copy = pltpu.make_async_remote_copy(
            src_ref=src, dst_ref=dst, send_sem=send_sem.at[k], recv_sem=recv_sem.at[k],
            device_id=device, device_id_type=pl.DeviceIdType.MESH,
        )
        copy.start()
        sent.append(copy)
        return copy

    barrier = pltpu.get_barrier_semaphore()
    for device in (core, cross, diag, side, near, far):
        pl.semaphore_signal(barrier, inc=1, device_id=device, device_id_type=pl.DeviceIdType.MESH)
    pl.semaphore_wait(barrier, 6)

    def rows_of(q):
        return pl.ds(pl.multiple_of(q * cap, 16), cap)

    def share_of(q):
        return pl.ds(pl.multiple_of(q * share, 16), share)

    tok = [
        send(pk.at[p2], x.at[t, rows_of(p)], cross),
        send(pk.at[p3], x.at[t, rows_of(p)], diag),
        send(pk.at[p1], x.at[t, rows_of(p)], core),
    ]
    loads = [
        pltpu.make_async_copy(pk.at[p], x.at[t, rows_of(p)], local_sem.at[0]),
        pltpu.make_async_copy(wup_hbm, wup, local_sem.at[1]),
        pltpu.make_async_copy(grad_hbm.at[0, share_of(p2)], g_own.at[0], local_sem.at[2]),
        pltpu.make_async_copy(wdown_hbm, wd.at[c], local_sem.at[3]),
        pltpu.make_async_copy(grad_hbm.at[0, share_of(p)], g_own.at[1], local_sem.at[4]),
    ]
    for load in loads:
        load.start()
    wd_core = send(wdown_hbm, wd.at[c], core)
    early = CHUNKS // 4

    def grad_to_core(first, end):
        start = pl.multiple_of(p3 * share + first * piece, 16)
        rows = pl.ds(start, (end - first) * piece)
        return send(grad_hbm.at[0, rows], g_near.at[0, pl.ds(first * piece, (end - first) * piece)], core)

    grad_first = grad_to_core(0, early)

    for copy in tok:
        copy.wait_recv()
    loads[0].wait()

    def pass_on(block, devices):
        return [send(x.at[block], x.at[block], device) for device in devices]

    tile = 512

    def project(s, e):
        block = 4 * e + 2 * (low if s in (0, 2) else 1 - low) + (y if s in (2, 3) else 1 - y)

        @pl.loop(0, 2)
        def _(part):
            for j in range(up.shape[5] // tile):
                start = pl.multiple_of(part * up.shape[5] + j * tile, tile)
                res = jnp.dot(x[block], wup[:, pl.ds(start, tile)], preferred_element_type=jnp.float32)
                res = res.astype(jnp.bfloat16)
                for q in range(n_dp):
                    up[part, q, s, e, :, j * tile : (j + 1) * tile] = res[
                        q * cap : (q + 1) * cap
                    ]

    def up_to_core(s):
        return [send(up.at[:, 1 - c + 2 * a, s], up_near.at[a, s], core) for a in range(2)]

    def up_to_cross(s):
        @pl.loop(0, 2)
        def _(m):
            for a in range(2):
                total = up[1 - h, c + 2 * a, s, m].astype(jnp.float32) + up_near[
                    a, s, 1 - h, m
                ].astype(jnp.float32)
                up[1 - h, c + 2 * a, s, m] = total.astype(jnp.bfloat16)

        return [send(up.at[1 - h, c + 2 * a, s], up_cross.at[a, s], cross) for a in range(2)]

    step = 32

    def pair_sum(first, end):
        @pl.loop(first * (piece // step), end * (piece // step))
        def _(i):
            rows = pl.ds(pl.multiple_of(i * step, step), step)
            total = g_own[0, rows].astype(jnp.float32) + g_near[0, rows].astype(jnp.float32)
            g_own[0, rows] = total.astype(jnp.bfloat16)

    def send_grad(k):
        rows = pl.ds(k * piece, piece)
        return send(g_own.at[0, rows], g_cross.at[rows], cross)

    own_far, own_near, own_side = pass_on(t, (far, near, side))
    loads[1].wait()
    project(2, high)
    own_far.wait_recv()
    far_near, far_side = pass_on(t4, (near, side))
    own_near.wait_recv()
    (near_side,) = pass_on(t2, (side,))
    project(2, other)
    far_near.wait_recv()
    (both_side,) = pass_on(flip(t2, 4), (side,))
    loads[2].wait()
    grad_first.wait_recv()
    pair_sum(0, early)
    grad_cross = [send_grad(k) for k in range(early)]

    own_side.wait_recv()
    project(0, high)
    far_side.wait_recv()
    project(0, other)
    core_0 = up_to_core(0)
    core_2 = up_to_core(2)
    project(3, high)
    for copy in core_0:
        copy.wait_recv()
    cross_0 = up_to_cross(0)
    project(3, other)
    core_3 = up_to_core(3)
    near_side.wait_recv()
    project(1, high)
    for copy in core_2:
        copy.wait_recv()
    cross_2 = up_to_cross(2)
    loads[3].wait()
    wd_core.wait_recv()
    width = 256

    def expert(s):
        @pl.loop(0, 2)
        def _(m):
            for a in range(2):
                pre = (
                    up[h, c + 2 * a, s, m].astype(jnp.float32)
                    + up_near[a, s, h, m].astype(jnp.float32)
                    + up_cross[a, s, m].astype(jnp.float32)
                )
                act = 0.5 * pre * (1.0 + lax.erf(pre * 0.7071067811865476))
                hid[rows_of(2 * m + a), :] = act.astype(jnp.bfloat16)

        @pl.loop(0, out.shape[4] // width)
        def _(j):
            cols = pl.ds(pl.multiple_of(j * width, width), width)
            weight = wd[:, :, cols].reshape(2 * share, width)
            res = jnp.dot(hid[...], weight, preferred_element_type=jnp.float32)
            out[s, :, :, :, cols] = res.reshape(2, 2, cap, width).astype(jnp.bfloat16)

    def send_out(s):
        return [send(out.at[s, e], from_y.at[2 * s + k], side) for k, e in enumerate((other, high))]

    for copy in cross_0:
        copy.wait_recv()
    expert(0)
    y_copies = send_out(0)
    both_side.wait_recv()
    project(1, other)
    core_1 = up_to_core(1)
    grad_rest = grad_to_core(early, CHUNKS)
    grad_last = send(grad_hbm.at[0, share_of(p1)], g_near.at[1], core)
    for copy in core_1:
        copy.wait_recv()
    cross_1 = up_to_cross(1)
    for copy in core_3:
        copy.wait_recv()
    cross_3 = up_to_cross(3)
    for copy in cross_2:
        copy.wait_recv()
    expert(2)
    for copy in cross_1:
        copy.wait_recv()
    expert(1)

    y_copies += send_out(1)
    grad_rest.wait_recv()
    for k in range(early, CHUNKS):
        pair_sum(k, k + 1)
        grad_cross.append(send_grad(k))
    for copy in cross_3:
        copy.wait_recv()
    expert(3)
    loads[4].wait()
    grad_last.wait_recv()

    def finish_grad(k):
        grad_cross[k].wait_recv()

        @pl.loop(0, piece // step)
        def _(i):
            rows = pl.ds(pl.multiple_of(k * piece + i * step, step), step)
            total = (
                g_own[1, rows].astype(jnp.float32)
                + g_near[1, rows].astype(jnp.float32)
                + g_cross[rows].astype(jnp.float32)
            )
            gsum[rows, :] = total.astype(jnp.bfloat16)

    def total_of(s, e, a, *others):
        total = out[s, e, a].astype(jnp.float32)
        for more in others:
            total += more[a].astype(jnp.float32)
        return total

    def merge(s, e, *others):
        for a in range(2):
            out[s, e, a] = total_of(s, e, a, *others).astype(jnp.bfloat16)

    y_copies[2].wait_recv()
    merge(3, other, from_y.at[2])
    z_first = send(out.at[3, other], from_z.at[0], near)
    for k in range(early):
        finish_grad(k)
    y_copies[3].wait_recv()
    merge(3, high, from_y.at[3])
    z_second = send(out.at[3, high], from_z.at[1], near)
    y_copies[0].wait_recv()
    z_first.wait_recv()
    merge(2, other, from_y.at[0], from_z.at[0])
    z_far = send(out.at[2, other], from_far, far)
    for k in range(early, CHUNKS // 2):
        finish_grad(k)
    y_copies[1].wait_recv()
    z_second.wait_recv()
    z_far.wait_recv()
    last = (from_y.at[1], from_z.at[1], from_far)
    fin_out[...] = total_of(2, high, 1 - h, *last).astype(jnp.bfloat16)
    fin = send(fin_out, fin_in, cross)
    for k in range(CHUNKS // 2, CHUNKS):
        finish_grad(k)
    fin.wait_recv()
    owned[...] = total_of(2, high, h, *last) + fin_in[...].astype(jnp.float32)

    for copy in sent:
        copy.wait_send()
    assert used[0] == send_sem.shape[0]


def layer(n_dp, n_tensor, pk, w_up, w_down, grad_parts):
    cap, depth = pk.shape[1:]
    hidden = w_up.shape[1]
    share, model = w_down.shape
    half = jnp.bfloat16
    copies = 38 + CHUNKS
    wide = (2, cap, hidden // 2)
    scratch = [
        pltpu.VMEM((n_tensor, n_dp * cap, depth), half),
        pltpu.VMEM((depth, hidden), half),
        pltpu.VMEM((2, n_dp, 4) + wide, half),
        pltpu.VMEM((2, 4, 2) + wide, half),
        pltpu.VMEM((2, 4) + wide, half),
        pltpu.VMEM((4 * cap, hidden // 2), half),
        pltpu.VMEM((2, share, model), half),
        pltpu.VMEM((4, 2, 2, cap, model), half),
        pltpu.VMEM((4, 2, cap, model), half),
        pltpu.VMEM((2, 2, cap, model), half),
        pltpu.VMEM((2, cap, model), half),
        pltpu.VMEM((cap, model), half),
        pltpu.VMEM((cap, model), half),
        pltpu.VMEM((2, share, model), half),
        pltpu.VMEM((2, share, model), half),
        pltpu.VMEM((share, model), half),
        pltpu.SemaphoreType.DMA((copies,)),
        pltpu.SemaphoreType.DMA((copies,)),
        pltpu.SemaphoreType.DMA((5,)),
    ]
    flops = 2 * n_tensor * n_dp * cap * depth * hidden + 2 * n_tensor * cap * hidden * model
    return pl.pallas_call(
        functools.partial(layer_kernel, n_dp, n_tensor),
        out_shape=(
            jax.ShapeDtypeStruct((cap, model), jnp.float32),
            jax.ShapeDtypeStruct((share, model), half),
        ),
        in_specs=[pl.BlockSpec(memory_space=pltpu.VMEM)] + [pl.BlockSpec(memory_space=pl.ANY)] * 3,
        out_specs=(pl.BlockSpec(memory_space=pltpu.VMEM), pl.BlockSpec(memory_space=pltpu.VMEM)),
        scratch_shapes=scratch,
        cost_estimate=pl.CostEstimate(
            flops=flops, bytes_accessed=40 * share * model, transcendentals=n_tensor * cap * hidden
        ),
        compiler_params=pltpu.CompilerParams(
            collective_id=0, has_side_effects=True, vmem_limit_bytes=VMEM_BYTES
        ),
    )(pk, w_up, w_down, grad_parts)


def local_kernel(n_dp, n_tensor, tokens, routes, router, w_up, w_down, grad_parts, master, moment_one, moment_two):
    routed, gating = gating_of(tokens, routes, router)
    slot_index = jnp.cumsum(routed.astype(jnp.int32)) - 1
    slot_iota = jnp.arange(CAP, dtype=jnp.int32)
    picks = ((slot_index[None, :] == slot_iota[:, None]) & routed[None, :]).astype(jnp.bfloat16)
    picked_rows = jnp.dot(picks, tokens, preferred_element_type=jnp.float32).astype(jnp.bfloat16)
    pk = picked_rows.reshape(CAP, n_dp, -1).transpose(1, 0, 2)
    owned, grad_total = layer(n_dp, n_tensor, pk, w_up, w_down, grad_parts)
    combined = jnp.take(owned, jnp.clip(slot_index, 0, CAP - 1), axis=0)
    mixed = (combined * gating[:, None]).astype(jnp.bfloat16)
    new_master, new_one, new_two = adam_step(
        grad_total.astype(jnp.float32), master, moment_one, moment_two
    )
    return (mixed, new_master, new_one, new_two)


def solution(mesh):
    placed = (
        P(("dp", "tensor"), None),
        P(("dp", "tensor"), None),
        P(),
        P("dp", "tensor"),
        P(("tensor", "dp"), None),
        P("dp", "tensor", None),
        P(("tensor", "dp"), None),
        P(("tensor", "dp"), None),
        P(("tensor", "dp"), None),
    )
    n_dp, n_tensor = mesh.shape["dp"], mesh.shape["tensor"]
    if (n_dp, n_tensor) == (4, 8):
        body = functools.partial(local_kernel, n_dp, n_tensor)
    else:
        body = local
    return jax.shard_map(
        body,
        mesh=mesh,
        in_specs=placed,
        out_specs=(
            P(("dp", "tensor"), None),
            P(("tensor", "dp"), None),
            P(("tensor", "dp"), None),
            P(("tensor", "dp"), None),
        ),
        check_vma=False,
    )
```

```python
import functools

import jax
import jax.numpy as jnp
from jax import lax
from jax.experimental import pallas as pl
from jax.experimental.pallas import tpu as pltpu
from jax.sharding import PartitionSpec as P

CAP = 48


beta_first = 0.9
beta_second = 0.999
learn_rate = 0.01
decay_rate = 0.1
adam_eps = 1e-08
bias_first = 1.0 - (0.9**10) ** 10
bias_second = 1.0 - (0.999**10) ** 10


def gating_of(tokens, routes, router):
    logits = jnp.dot(tokens, router, preferred_element_type=jnp.float32)
    expert_iota = jnp.arange(logits.shape[1], dtype=jnp.int32)
    chosen = jnp.sum(jnp.where(routes[:, :, None] == expert_iota, logits[:, None, :], 0.0), axis=2)
    is_first = routes[:, 0] == 0
    routed = is_first | (routes[:, 1] == 0)
    own_logit = jnp.where(is_first, chosen[:, 0], chosen[:, 1])
    partner = jnp.where(is_first, chosen[:, 1], chosen[:, 0])
    gating = jnp.where(routed, jax.nn.sigmoid(own_logit - partner), 0.0)
    return (routed, gating)


def adam_step(grad_total, master, moment_one, moment_two):
    new_one = (
        beta_first * moment_one.astype(jnp.float32) + (1.0 - beta_first) * grad_total
    ).astype(jnp.bfloat16)
    new_two = beta_second * moment_two + (1.0 - beta_second) * grad_total * grad_total
    update = new_one.astype(jnp.float32) / bias_first / (jnp.sqrt(new_two / bias_second) + adam_eps)
    new_master = master - learn_rate * (update + decay_rate * master)
    return (new_master, new_one, new_two)


def local(tokens, routes, router, w_up, w_down, grad_parts, master, moment_one, moment_two):
    routed, gating = gating_of(tokens, routes, router)
    slot_index = jnp.cumsum(routed.astype(jnp.int32)) - 1
    slot_iota = jnp.arange(CAP, dtype=jnp.int32)
    picks = ((slot_index[None, :] == slot_iota[:, None]) & routed[None, :]).astype(jnp.bfloat16)
    picked_rows = jnp.dot(picks, tokens, preferred_element_type=jnp.float32).astype(jnp.bfloat16)
    gathered = lax.all_gather(picked_rows, "tensor", axis=0, tiled=True)
    up_out = jnp.dot(
        gathered, lax.all_gather(w_up, "dp", axis=0, tiled=True), preferred_element_type=jnp.float32
    )
    hidden = jax.nn.gelu(up_out, approximate=False).astype(jnp.bfloat16)
    partials = jnp.dot(
        hidden, lax.all_gather(w_down, "dp", axis=0, tiled=True), preferred_element_type=jnp.float32
    )
    owned = lax.psum_scatter(
        partials.astype(jnp.bfloat16), "tensor", scatter_dimension=0, tiled=True
    ).astype(jnp.float32)
    combined = jnp.take(owned, jnp.clip(slot_index, 0, CAP - 1), axis=0)
    mixed = (combined * gating[:, None]).astype(jnp.bfloat16)
    local_grad = grad_parts[0]
    grad_total = lax.psum_scatter(local_grad, "dp", scatter_dimension=0, tiled=True).astype(
        jnp.float32
    )
    new_master, new_one, new_two = adam_step(grad_total, master, moment_one, moment_two)
    return (mixed, new_master, new_one, new_two)


CHUNKS = 8
VMEM_BYTES = 60 * 1024 * 1024


def flip(index, bit):
    return index + bit - 2 * bit * lax.rem(lax.div(index, bit), 2)


def layer_kernel(
    n_dp, n_tensor, pk, wup_hbm, wdown_hbm, grad_hbm,
    owned, gsum,
    x, wup, up, up_near, up_cross, hid, wd, out, from_y, from_z, from_far, fin_out, fin_in,
    g_own, g_near, g_cross, send_sem, recv_sem, local_sem,
):
    p = lax.axis_index("dp")
    t = lax.axis_index("tensor")
    c, h = lax.rem(p, 2), lax.div(p, 2)
    y, low, high = lax.rem(t, 2), lax.rem(lax.div(t, 2), 2), lax.div(t, 4)
    other = 1 - high
    p1, p2 = flip(p, 1), flip(p, 2)
    p3 = flip(p1, 2)
    t1, t2, t4 = flip(t, 1), flip(t, 2), flip(t, 4)
    core, cross, diag = (p1, t), (p2, t), (p3, t)
    side, near, far = (p, t1), (p, t2), (p, t4)
    cap = pk.shape[1]
    share = wdown_hbm.shape[0]
    piece = share // CHUNKS
    used = [0]
    sent = []

    def send(src, dst, device):
        k = used[0]
        used[0] += 1
        copy = pltpu.make_async_remote_copy(
            src_ref=src, dst_ref=dst, send_sem=send_sem.at[k], recv_sem=recv_sem.at[k],
            device_id=device, device_id_type=pl.DeviceIdType.MESH,
        )
        copy.start()
        sent.append(copy)
        return copy

    barrier = pltpu.get_barrier_semaphore()
    for device in (core, cross, diag, side, near, far):
        pl.semaphore_signal(barrier, inc=1, device_id=device, device_id_type=pl.DeviceIdType.MESH)
    pl.semaphore_wait(barrier, 6)

    def rows_of(q):
        return pl.ds(pl.multiple_of(q * cap, 16), cap)

    def share_of(q):
        return pl.ds(pl.multiple_of(q * share, 16), share)

    tok = [
        send(pk.at[p2], x.at[t, rows_of(p)], cross),
        send(pk.at[p3], x.at[t, rows_of(p)], diag),
        send(pk.at[p1], x.at[t, rows_of(p)], core),
    ]
    loads = [
        pltpu.make_async_copy(pk.at[p], x.at[t, rows_of(p)], local_sem.at[0]),
        pltpu.make_async_copy(wup_hbm, wup, local_sem.at[1]),
        pltpu.make_async_copy(grad_hbm.at[0, share_of(p2)], g_own.at[0], local_sem.at[2]),
        pltpu.make_async_copy(wdown_hbm, wd.at[c], local_sem.at[3]),
        pltpu.make_async_copy(grad_hbm.at[0, share_of(p)], g_own.at[1], local_sem.at[4]),
    ]
    for load in loads:
        load.start()
    wd_core = send(wdown_hbm, wd.at[c], core)
    early = CHUNKS // 4

    def grad_to_core(first, end):
        start = pl.multiple_of(p3 * share + first * piece, 16)
        rows = pl.ds(start, (end - first) * piece)
        return send(grad_hbm.at[0, rows], g_near.at[0, pl.ds(first * piece, (end - first) * piece)], core)

    grad_first = grad_to_core(0, early)

    for copy in tok:
        copy.wait_recv()
    loads[0].wait()

    def pass_on(block, devices):
        return [send(x.at[block], x.at[block], device) for device in devices]

    tile = 512

    def project(s, e):
        block = 4 * e + 2 * (low if s in (0, 2) else 1 - low) + (y if s in (2, 3) else 1 - y)

        @pl.loop(0, 2)
        def _(part):
            for j in range(up.shape[5] // tile):
                start = pl.multiple_of(part * up.shape[5] + j * tile, tile)
                res = jnp.dot(x[block], wup[:, pl.ds(start, tile)], preferred_element_type=jnp.float32)
                res = res.astype(jnp.bfloat16)
                for q in range(n_dp):
                    up[part, q, s, e, :, j * tile : (j + 1) * tile] = res[
                        q * cap : (q + 1) * cap
                    ]

    def up_to_core(s):
        return [send(up.at[:, 1 - c + 2 * a, s], up_near.at[a, s], core) for a in range(2)]

    def up_to_cross(s):
        @pl.loop(0, 2)
        def _(m):
            for a in range(2):
                total = up[1 - h, c + 2 * a, s, m].astype(jnp.float32) + up_near[
                    a, s, 1 - h, m
                ].astype(jnp.float32)
                up[1 - h, c + 2 * a, s, m] = total.astype(jnp.bfloat16)

        return [send(up.at[1 - h, c + 2 * a, s], up_cross.at[a, s], cross) for a in range(2)]

    step = 32

    def pair_sum(first, end):
        @pl.loop(first * (piece // step), end * (piece // step))
        def _(i):
            rows = pl.ds(pl.multiple_of(i * step, step), step)
            total = g_own[0, rows].astype(jnp.float32) + g_near[0, rows].astype(jnp.float32)
            g_own[0, rows] = total.astype(jnp.bfloat16)

    def send_grad(k):
        rows = pl.ds(k * piece, piece)
        return send(g_own.at[0, rows], g_cross.at[rows], cross)

    own_far, own_near, own_side = pass_on(t, (far, near, side))
    loads[1].wait()
    project(2, high)
    own_far.wait_recv()
    far_near, far_side = pass_on(t4, (near, side))
    own_near.wait_recv()
    (near_side,) = pass_on(t2, (side,))
    project(2, other)
    far_near.wait_recv()
    (both_side,) = pass_on(flip(t2, 4), (side,))
    loads[2].wait()
    grad_first.wait_recv()
    pair_sum(0, early)
    grad_cross = [send_grad(k) for k in range(early)]

    own_side.wait_recv()
    project(0, high)
    far_side.wait_recv()
    project(0, other)
    core_0 = up_to_core(0)
    core_2 = up_to_core(2)
    project(3, high)
    for copy in core_0:
        copy.wait_recv()
    cross_0 = up_to_cross(0)
    project(3, other)
    core_3 = up_to_core(3)
    grad_rest = grad_to_core(early, CHUNKS)
    grad_last = send(grad_hbm.at[0, share_of(p1)], g_near.at[1], core)
    near_side.wait_recv()
    project(1, high)
    for copy in core_2:
        copy.wait_recv()
    cross_2 = up_to_cross(2)
    loads[3].wait()
    wd_core.wait_recv()
    width = 256

    def expert(s):
        @pl.loop(0, 2)
        def _(m):
            for a in range(2):
                pre = (
                    up[h, c + 2 * a, s, m].astype(jnp.float32)
                    + up_near[a, s, h, m].astype(jnp.float32)
                    + up_cross[a, s, m].astype(jnp.float32)
                )
                act = 0.5 * pre * (1.0 + lax.erf(pre * 0.7071067811865476))
                hid[rows_of(2 * m + a), :] = act.astype(jnp.bfloat16)

        @pl.loop(0, out.shape[4] // width)
        def _(j):
            cols = pl.ds(pl.multiple_of(j * width, width), width)
            weight = wd[:, :, cols].reshape(2 * share, width)
            res = jnp.dot(hid[...], weight, preferred_element_type=jnp.float32)
            out[s, :, :, :, cols] = res.reshape(2, 2, cap, width).astype(jnp.bfloat16)

    def send_out(s):
        return [
            send(out.at[s, e, a], from_y.at[2 * s + k, a], side)
            for k, e in enumerate((other, high))
            for a in (1 - h, h)
        ]

    for copy in cross_0:
        copy.wait_recv()
    expert(0)
    y_copies = send_out(0)
    both_side.wait_recv()
    project(1, other)
    core_1 = up_to_core(1)
    for copy in core_1:
        copy.wait_recv()
    cross_1 = up_to_cross(1)
    for copy in core_3:
        copy.wait_recv()
    cross_3 = up_to_cross(3)
    for copy in cross_2:
        copy.wait_recv()
    expert(2)
    grad_rest.wait_recv()
    pair_sum(early, 2 * early)
    for copy in cross_1:
        copy.wait_recv()
    for k in range(early, 2 * early):
        grad_cross.append(send_grad(k))
    expert(1)

    y_copies += send_out(1)
    for k in range(2 * early, CHUNKS):
        pair_sum(k, k + 1)
        grad_cross.append(send_grad(k))
    for copy in cross_3:
        copy.wait_recv()
    expert(3)
    loads[4].wait()
    grad_last.wait_recv()

    def finish_grad(k):
        grad_cross[k].wait_recv()

        @pl.loop(0, piece // step)
        def _(i):
            rows = pl.ds(pl.multiple_of(k * piece + i * step, step), step)
            total = (
                g_own[1, rows].astype(jnp.float32)
                + g_near[1, rows].astype(jnp.float32)
                + g_cross[rows].astype(jnp.float32)
            )
            gsum[rows, :] = total.astype(jnp.bfloat16)

    def total_of(s, e, a, *others):
        total = out[s, e, a].astype(jnp.float32)
        for more in others:
            total += more[a].astype(jnp.float32)
        return total

    def merge(s, e, a, *others):
        out[s, e, a] = total_of(s, e, a, *others).astype(jnp.bfloat16)

    def to_near(slot, e, a):
        merge(3, e, a, from_y.at[2 + slot])
        return send(out.at[3, e, a], from_z.at[slot, a], near)

    def to_far(a):
        merge(2, other, a, from_y.at[0], from_z.at[0])
        return send(out.at[2, other, a], from_far.at[a], far)

    first, second = 1 - h, h
    y_copies[4].wait_recv()
    z_first = [to_near(0, other, first)]
    y_copies[5].wait_recv()
    z_first.append(to_near(0, other, second))
    y_copies[0].wait_recv()
    y_copies[1].wait_recv()
    z_first[0].wait_recv()
    z_far = [to_far(first)]
    y_copies[6].wait_recv()
    z_second = [to_near(1, high, first)]
    z_first[1].wait_recv()
    z_far.append(to_far(second))
    y_copies[7].wait_recv()
    z_second.append(to_near(1, high, second))
    for k in range(2 * early):
        finish_grad(k)
    y_copies[2].wait_recv()
    y_copies[3].wait_recv()
    last = (from_y.at[1], from_z.at[1], from_far)
    z_second[0].wait_recv()
    z_far[0].wait_recv()
    fin_out[...] = total_of(2, high, first, *last).astype(jnp.bfloat16)
    fin = send(fin_out, fin_in, cross)
    for k in range(2 * early, CHUNKS):
        finish_grad(k)
    z_second[1].wait_recv()
    z_far[1].wait_recv()
    fin.wait_recv()
    owned[...] = total_of(2, high, second, *last) + fin_in[...].astype(jnp.float32)

    for copy in sent:
        copy.wait_send()
    assert used[0] == send_sem.shape[0]


def layer(n_dp, n_tensor, pk, w_up, w_down, grad_parts):
    cap, depth = pk.shape[1:]
    hidden = w_up.shape[1]
    share, model = w_down.shape
    half = jnp.bfloat16
    copies = 45 + CHUNKS
    wide = (2, cap, hidden // 2)
    scratch = [
        pltpu.VMEM((n_tensor, n_dp * cap, depth), half),
        pltpu.VMEM((depth, hidden), half),
        pltpu.VMEM((2, n_dp, 4) + wide, half),
        pltpu.VMEM((2, 4, 2) + wide, half),
        pltpu.VMEM((2, 4) + wide, half),
        pltpu.VMEM((4 * cap, hidden // 2), half),
        pltpu.VMEM((2, share, model), half),
        pltpu.VMEM((4, 2, 2, cap, model), half),
        pltpu.VMEM((4, 2, cap, model), half),
        pltpu.VMEM((2, 2, cap, model), half),
        pltpu.VMEM((2, cap, model), half),
        pltpu.VMEM((cap, model), half),
        pltpu.VMEM((cap, model), half),
        pltpu.VMEM((2, share, model), half),
        pltpu.VMEM((2, share, model), half),
        pltpu.VMEM((share, model), half),
        pltpu.SemaphoreType.DMA((copies,)),
        pltpu.SemaphoreType.DMA((copies,)),
        pltpu.SemaphoreType.DMA((5,)),
    ]
    flops = 2 * n_tensor * n_dp * cap * depth * hidden + 2 * n_tensor * cap * hidden * model
    return pl.pallas_call(
        functools.partial(layer_kernel, n_dp, n_tensor),
        out_shape=(
            jax.ShapeDtypeStruct((cap, model), jnp.float32),
            jax.ShapeDtypeStruct((share, model), half),
        ),
        in_specs=[pl.BlockSpec(memory_space=pltpu.VMEM)] + [pl.BlockSpec(memory_space=pl.ANY)] * 3,
        out_specs=(pl.BlockSpec(memory_space=pltpu.VMEM), pl.BlockSpec(memory_space=pltpu.VMEM)),
        scratch_shapes=scratch,
        cost_estimate=pl.CostEstimate(
            flops=flops, bytes_accessed=40 * share * model, transcendentals=n_tensor * cap * hidden
        ),
        compiler_params=pltpu.CompilerParams(
            collective_id=0, has_side_effects=True, vmem_limit_bytes=VMEM_BYTES
        ),
    )(pk, w_up, w_down, grad_parts)


def local_kernel(n_dp, n_tensor, tokens, routes, router, w_up, w_down, grad_parts, master, moment_one, moment_two):
    routed, gating = gating_of(tokens, routes, router)
    slot_index = jnp.cumsum(routed.astype(jnp.int32)) - 1
    slot_iota = jnp.arange(CAP, dtype=jnp.int32)
    picks = ((slot_index[None, :] == slot_iota[:, None]) & routed[None, :]).astype(jnp.bfloat16)
    picked_rows = jnp.dot(picks, tokens, preferred_element_type=jnp.float32).astype(jnp.bfloat16)
    pk = picked_rows.reshape(CAP, n_dp, -1).transpose(1, 0, 2)
    owned, grad_total = layer(n_dp, n_tensor, pk, w_up, w_down, grad_parts)
    combined = lax.dot_general(
        picks.astype(jnp.float32), owned, (((0,), (0,)), ((), ())), precision=lax.Precision.HIGHEST
    )
    mixed = (combined * gating[:, None]).astype(jnp.bfloat16)
    new_master, new_one, new_two = adam_step(
        grad_total.astype(jnp.float32), master, moment_one, moment_two
    )
    return (mixed, new_master, new_one, new_two)


def solution(mesh):
    placed = (
        P(("dp", "tensor"), None),
        P(("dp", "tensor"), None),
        P(),
        P("dp", "tensor"),
        P(("tensor", "dp"), None),
        P("dp", "tensor", None),
        P(("tensor", "dp"), None),
        P(("tensor", "dp"), None),
        P(("tensor", "dp"), None),
    )
    n_dp, n_tensor = mesh.shape["dp"], mesh.shape["tensor"]
    if (n_dp, n_tensor) == (4, 8):
        body = functools.partial(local_kernel, n_dp, n_tensor)
    else:
        body = local
    return jax.shard_map(
        body,
        mesh=mesh,
        in_specs=placed,
        out_specs=(
            P(("dp", "tensor"), None),
            P(("tensor", "dp"), None),
            P(("tensor", "dp"), None),
            P(("tensor", "dp"), None),
        ),
        check_vma=False,
    )
```
